1024 devices in a mesh: section: 16 (over x, y_hi), ep: 64 (over z, y_lo, core).
Axes of the slice: x: 4, y: 8 (y_hi: 4, y_lo: 2; y = y_hi * 2 + y_lo), z: 16, core: 2. Of those that a mesh axis runs over, the one named last changes fastest.
Arguments:
- tokens_a: bfloat16 [4096, 3584], P(('section', 'ep')), may hold values from -6 to 6
- tokens_b: bfloat16 [4096, 3584], P(('section', 'ep')), may hold values from -6 to 6
- routes_a: int32 [4096, 2], P(('section', 'ep')), may hold values from 0 to 3, all different within a row; in each aligned block of 4 rows (0 to 3, 4 to 7, ...) at most 2 rows name the same one
- routes_b: int32 [4096, 2], P(('section', 'ep')), may hold values from 0 to 3, all different within a row; in each aligned block of 4 rows (0 to 3, 4 to 7, ...) at most 2 rows name the same one
- gains_a: float32 [4096, 2], P(('section', 'ep')), may hold values from 0.3 to 1.5
- gains_b: float32 [4096, 2], P(('section', 'ep')), may hold values from 0.3 to 1.5
- w_gate_up: bfloat16 [16, 3584, 2, 8192], P('section', None, None, 'ep'), may hold values from -0.09375 to 0.09375
- w_down: bfloat16 [16, 8192, 3584], P('section', 'ep'), may hold values from -0.125 to 0.125
Outputs:
- mixed_a: bfloat16 [4096, 3584], P(('section', 'ep'))
- mixed_b: bfloat16 [4096, 3584], P(('section', 'ep'))
The draws below stay inside these ranges and needn't reach their ends.
Inputs may be any that keep to these rules, and one draw needn't show every extreme that they name: `routes_a`: each row names 2 different experts. Among the 4 rows of one device, no expert is named more than 2 times, and in every draw some device's rows name some expert exactly 2 times. `routes_b`: as for routes_a.
All inputs are finite; a program needn't handle non-finite values.
Results may differ from the reference program's by a relative error of at most 0.0065.
Values may be sent and summed in bfloat16 or wider, within the bound.
A program may use at most 32 MiB of HBM per device.

```python
import math
import jax
import jax.numpy as jnp
import numpy as np
from jax import lax

D = 3584
FF = 2048
EXPERTS = 4
TOP = 2
TOK_DEV = 4
CAP = 2
GROUP = 16
FF_DEV = 128
ROWS = 4096
N_SECTION = 16
N_EP = 64


def steps_of(stream_key, dims, cuts, low, largest):
    loudness, own = 1.0, jax.random.fold_in(stream_key, 6)
    for dim, blocks in cuts:
        steps = jnp.exp(jax.random.uniform(jax.random.fold_in(own, dim), (blocks,), jnp.float32, low / len(cuts), largest / len(cuts)))
        loudness = loudness * jnp.repeat(steps, dims[dim] // blocks).reshape([-1 if axis == dim else 1 for axis in range(len(dims))])
    return loudness


def deal_out(key, own, number, rows, count, top, most, lean):
    sequence = jax.random.permutation(key, count)
    heavy_load, usual = shares(count, rows * top, most, lean, True), shares(count, rows * top, most, lean, False)
    places = jnp.arange(count)

    def named(sizes, offset_by):
        used = int((sizes > 0).sum())
        fixed = max(1, used // 4)
        shifted = fixed + (places - fixed + offset_by * (used - fixed)) % max(1, count - fixed)
        return jnp.zeros((count,), jnp.int32).at[sequence[jnp.where(places < fixed, places, shifted)]].set(jnp.asarray(sizes, jnp.int32))

    sizes = jnp.where(number % 4 == 0, named(heavy_load, number // 4), named(usual, number - number // 4 - 1))
    mixed = jax.random.permutation(jax.random.fold_in(own, 3), count)
    donor, receiver = mixed[0:count // 2 * 2:2], mixed[1:count // 2 * 2:2]
    slack = jnp.minimum(sizes[donor] - 1, most - sizes[receiver]) // 2
    slack = jnp.where((donor == sequence[0]) | (receiver == sequence[0]) | (sizes[receiver] == 0), 0, jnp.maximum(slack, 0))
    shifted = jax.random.randint(jax.random.fold_in(own, 4), (count // 2,), 0, 1 << 20) % (slack + 1)
    sizes = sizes.at[donor].add(-shifted).at[receiver].add(shifted)
    items = jnp.searchsorted(jnp.cumsum(sizes), jnp.arange(rows * top), side="right").astype(jnp.int32)
    listing = items.reshape(top, rows).T
    listing = listing[jax.random.permutation(jax.random.fold_in(own, 1), rows)]
    offset_by = jax.random.randint(jax.random.fold_in(own, 2), (rows, 1), 0, top)
    return jnp.take_along_axis(listing, (jnp.arange(top)[None, :] + offset_by) % top, axis=1)


def shares(amount, total, bound, lean, full):
    portions = [(1 << 20) // math.isqrt(standing ** lean) + 1 for standing in range(1, amount + 1)]
    largest = bound if full else min(bound, max(-(-total // amount), total * portions[0] // sum(portions)))
    least = 1 if total - largest >= amount - 1 else 0
    counts, spare = [largest] + [least] * (amount - 1), total - largest - least * (amount - 1)
    while spare > 0:
        candidates = [i for i in range(1, amount) if counts[i] < largest] or [i for i in range(1, amount) if counts[i] < bound]
        pool, budget = sum([portions[i] for i in candidates]), spare
        for i in candidates:
            addition = min(bound - counts[i], max(1, budget * portions[i] // pool), spare)
            counts[i] = counts[i] + addition
            spare = spare - addition
    return np.array(counts)


def noise(key, extent, width, most, pieces=(), kind=jnp.bfloat16):
    drawn = jax.random.normal(key, extent, jnp.float32) * width
    if len(pieces) > 0:
        drawn = steps_of(key, extent, pieces, -0.22, 0.18) * drawn
    return jnp.clip(drawn, min=-most, max=most).astype(kind)


def setup_inputs(seed: int = 0) -> dict:
    arg_keys = jax.random.split(jax.random.key(seed), 9)
    tokens_a = noise(arg_keys[0], (ROWS, D), 1.0, 6.0, ((0, 1024),))
    tokens_b = noise(arg_keys[1], (ROWS, D), 1.0, 6.0, ((0, 1024),))
    routes_a_keys = jax.random.split(jax.random.fold_in(arg_keys[2], 1), ROWS // TOK_DEV)
    routes_a_turns = jax.random.permutation(jax.random.fold_in(arg_keys[2], 3), ROWS // TOK_DEV)
    routes_a = jax.vmap(lambda own, number: deal_out(jax.random.fold_in(arg_keys[2], 2), own, number, TOK_DEV, EXPERTS, TOP, CAP, 2))(routes_a_keys, routes_a_turns).reshape((ROWS, TOP))
    routes_b_keys = jax.random.split(jax.random.fold_in(arg_keys[3], 1), ROWS // TOK_DEV)
    routes_b_turns = jax.random.permutation(jax.random.fold_in(arg_keys[3], 3), ROWS // TOK_DEV)
    routes_b = jax.vmap(lambda own, number: deal_out(jax.random.fold_in(arg_keys[3], 2), own, number, TOK_DEV, EXPERTS, TOP, CAP, 2))(routes_b_keys, routes_b_turns).reshape((ROWS, TOP))
    gains_a = jnp.clip(0.3 + 1.2 * jax.random.uniform(arg_keys[4], (ROWS, TOP), jnp.float32) ** steps_of(arg_keys[4], (ROWS, TOP), ((0, 1024),), -0.2, 0.2), 0.3, 1.5)
    gains_b = jnp.clip(0.3 + 1.2 * jax.random.uniform(arg_keys[5], (ROWS, TOP), jnp.float32) ** steps_of(arg_keys[5], (ROWS, TOP), ((0, 1024),), -0.2, 0.2), 0.3, 1.5)
    w_gate_up = noise(arg_keys[6], (N_SECTION, D, 2, EXPERTS * FF), D ** -0.5, 0.09375, ((0, 16), (3, 64)))
    w_down = noise(arg_keys[7], (N_SECTION, EXPERTS * FF, D), FF ** -0.5, 0.125, ((0, 16), (1, 64)))
    return dict(tokens_a=tokens_a, tokens_b=tokens_b, routes_a=routes_a, routes_b=routes_b, gains_a=gains_a, gains_b=gains_b, w_gate_up=w_gate_up, w_down=w_down)


def route_slots(routes_flat):
    onehot = (routes_flat[:, None] == jnp.arange(EXPERTS, dtype=jnp.int32)[None, :]).astype(jnp.int32)
    return jnp.sum((jnp.cumsum(onehot, axis=0) - 1) * onehot, axis=1).astype(jnp.int32)


def section_layer(current, routes, gains, gate_up, down):
    per_device = routes.reshape(N_EP, TOK_DEV * TOP)
    slot_ids = jax.vmap(route_slots)(per_device)
    source = jnp.arange(N_EP, dtype=jnp.int32)[:, None]
    position = (source * CAP + slot_ids).reshape(-1)
    choice_idx = jnp.arange(TOK_DEV * TOP, dtype=jnp.int32)[None, :]
    token_idx = (source * TOK_DEV + choice_idx // TOP).reshape(-1)
    expert_ids = per_device.reshape(-1)
    buffer = jnp.zeros((EXPERTS, N_EP * CAP, D), jnp.bfloat16)
    buffer = buffer.at[expert_ids, position].set(current[token_idx])

    def one_expert(index):
        cols = lax.dynamic_slice_in_dim(gate_up, index * FF, FF, 2).reshape(D, 2 * FF)
        rows_down = lax.dynamic_slice_in_dim(down, index * FF, FF, 0)
        inputs = lax.dynamic_index_in_dim(buffer, index, 0, keepdims=False)
        projected = jnp.dot(inputs, cols, preferred_element_type=jnp.float32)
        hidden = (jax.nn.silu(projected[:, :FF]) * projected[:, FF:]).astype(jnp.bfloat16)
        partial_value = jnp.einsum("rgf,gfd->rgd", hidden.reshape(-1, GROUP, FF_DEV).astype(jnp.float32),
                             rows_down.reshape(GROUP, FF_DEV, D).astype(jnp.float32))
        partial_value = lax.optimization_barrier(partial_value.astype(jnp.bfloat16))
        return jnp.sum(partial_value.astype(jnp.float32), axis=1)

    expert_out = lax.map(one_expert, jnp.arange(EXPERTS, dtype=jnp.int32))
    routed = expert_out[expert_ids, position].reshape(N_EP * TOK_DEV, TOP, D)
    mixed = current.astype(jnp.float32) + jnp.sum(gains[:, :, None] * routed, axis=1)
    return mixed.astype(jnp.bfloat16)


def run_stream(tokens, routes, gains, w_gate_up, w_down, forward):
    blocks = tokens.reshape(N_SECTION, N_EP * TOK_DEV, D)
    if forward:
        current = jnp.concatenate([blocks[:1], blocks[:-1]], axis=0)
    else:
        current = jnp.concatenate([blocks[1:], blocks[-1:]], axis=0)
    routes_s = routes.reshape(N_SECTION, N_EP * TOK_DEV, TOP)
    gains_s = gains.reshape(N_SECTION, N_EP * TOK_DEV, TOP)

    def one_section(items):
        return section_layer(*items)

    mixed = lax.map(one_section, (current, routes_s, gains_s, w_gate_up, w_down))
    return mixed.reshape(ROWS, D)


def reference(tokens_a, tokens_b, routes_a, routes_b, gains_a, gains_b, w_gate_up, w_down):
    mixed_a = run_stream(tokens_a, routes_a, gains_a, w_gate_up, w_down, True)
    mixed_b = run_stream(tokens_b, routes_b, gains_b, w_gate_up, w_down, False)
    return mixed_a, mixed_b
```

```python
import functools

import jax
import jax.numpy as jnp
from jax import lax
from jax.experimental import pallas as pl
from jax.experimental.pallas import tpu as pltpu
from jax.sharding import PartitionSpec as P

EXPERTS = 4
TOP = 2
TOK = 4
CAP = 2
QUARTERS = 4
PER_GROUP = 4
LEAD = 2
BF16 = jnp.bfloat16
F32 = jnp.float32


def slot_order(nz):
    order = [0]
    for step in range(1, nz // 2):
        order += [step, nz - step]
    return order + [nz // 2]


class Copies:
    def __init__(self, send_sems, recv_sems):
        self.send_sems, self.recv_sems, self.used = send_sems, recv_sems, 0

    def make(self, src, dst, device):
        index = self.used
        self.used += 1
        return pltpu.make_async_remote_copy(
            src_ref=src,
            dst_ref=dst,
            send_sem=self.send_sems.at[index],
            recv_sem=self.recv_sems.at[index],
            device_id=device,
            device_id_type=pl.DeviceIdType.MESH,
        )


def n_copies(nz):
    half, groups = nz // 2, nz // PER_GROUP
    ring = 2 * (2 * half - 1)
    return 2 + (2 * half - 1) + 2 * ring + 3 * groups + 2 * groups


def iota(shape, dim):
    return lax.broadcasted_iota(jnp.int32, shape, dim)


def kernel(
    ns,
    nz,
    d,
    tok_a,
    tok_b,
    routes_a,
    routes_b,
    gains_a,
    gains_b,
    wgu_hbm,
    wd_hbm,
    out_a,
    out_b,
    outgoing,
    ring,
    meta,
    x,
    wgu_raw,
    wgu,
    wd,
    p_own,
    p_send,
    p_recv,
    y_send,
    y_recv,
    expand,
    gain_col,
    contrib,
    rs_send,
    rs_recv,
    send_sems,
    recv_sems,
    local_sems,
):
    q = d // QUARTERS
    half = nz // 2
    groups = nz // PER_GROUP
    order = slot_order(nz)
    pos = {r: i for i, r in enumerate(order)}

    section = lax.axis_index("section")
    ep = lax.axis_index("ep")
    z, low = ep // 4, ep % 4
    y, core = low // 2, low % 2
    expert = z // (nz // EXPERTS)
    right = (section, lax.rem(z + 1, nz) * 4 + low)
    left = (section, lax.rem(z + nz - 1, nz) * 4 + low)
    across = (section, ep + 2 - 4 * y)
    twin = (section, ep + 1 - 2 * core)
    up = (section + 1, ep)
    down = (section - 1, ep)
    not_last = section < ns - 1
    not_first = section > 0

    load_gu = pltpu.make_async_copy(wgu_hbm.at[0], wgu_raw, local_sems.at[0])
    load_d = pltpu.make_async_copy(wd_hbm.at[0], wd, local_sems.at[1])
    load_gu.start()
    load_d.start()

    barrier = pltpu.get_barrier_semaphore()
    for peer in (right, left, across, twin):
        pl.semaphore_signal(barrier, inc=1, device_id=peer, device_id_type=pl.DeviceIdType.MESH)

    @pl.when(not_last)
    def _():
        pl.semaphore_signal(barrier, inc=1, device_id=up, device_id_type=pl.DeviceIdType.MESH)

    @pl.when(not_first)
    def _():
        pl.semaphore_signal(barrier, inc=1, device_id=down, device_id_type=pl.DeviceIdType.MESH)

    for stream, tok in enumerate((tok_a, tok_b)):
        rows = tok[...].astype(F32)
        outgoing[stream] = jnp.concatenate(
            [rows[:, i * q : (i + 1) * q] for i in range(QUARTERS)], axis=0
        ).astype(BF16)

    lane = iota((1, 128), 1)
    lane_stream = (lane // 8) % 2
    lane_expert = (lane // CAP) % EXPERTS
    lane_slot = lane % CAP
    count = jnp.zeros((1, 128), jnp.int32)
    token = jnp.zeros((1, 128), F32)
    gain = jnp.zeros((1, 128), F32)
    for t in range(TOK):
        for k in range(TOP):
            route = jnp.where(lane_stream == 0, routes_a[t, k], routes_b[t, k])
            value = jnp.where(lane_stream == 0, gains_a[t, k], gains_b[t, k])
            named = route == lane_expert
            here = named & (count == lane_slot)
            token = jnp.where(here, float(t), token)
            gain = jnp.where(here, value, gain)
            count = count + named.astype(jnp.int32)
    meta[0] = jnp.where(lane < 16, token, gain)

    copies = Copies(send_sems, recv_sems)
    relay_up = copies.make(outgoing.at[0], ring.at[0, 0], up)
    relay_down = copies.make(outgoing.at[1], ring.at[0, 1], down)
    plus, minus = [{}, {}], [{}, {}]
    for j in range(1, half + 1):
        for s in range(2):
            if j < half or s == 0:
                plus[s][j] = copies.make(ring.at[pos[j - 1], s], ring.at[pos[j], s], right)
            if j < half or s == 1:
                minus[s][j] = copies.make(
                    ring.at[pos[(nz - j + 1) % nz], s], ring.at[pos[nz - j], s], left
                )
    meta_plus, meta_minus = {}, {}
    for j in range(1, half + 1):
        meta_plus[j] = copies.make(meta.at[pos[j - 1]], meta.at[pos[j]], right)
        if j < half:
            meta_minus[j] = copies.make(meta.at[pos[(nz - j + 1) % nz]], meta.at[pos[nz - j]], left)

    x_across = [copies.make(x.at[k, 0], x.at[k, 2], across) for k in range(groups)]
    x_twin = [copies.make(x.at[k, 0], x.at[k, 1], twin) for k in range(groups)]
    x_far = [copies.make(x.at[k, 2], x.at[k, 3], twin) for k in range(groups)]
    p_twin = [copies.make(p_send.at[k], p_recv.at[k], twin) for k in range(groups)]
    p_across = [copies.make(y_send.at[k], y_recv.at[k], across) for k in range(groups)]
    back = [[{}, {}], [{}, {}]]
    for j in range(1, half + 1):
        for way, device in enumerate((right, left)):
            for s in range(2):
                if j > 1 or s == way:
                    back[way][s][j] = copies.make(
                        rs_send.at[way, j - 1, s], rs_recv.at[way, j - 1, s], device
                    )

    pl.semaphore_wait(barrier, 4 + not_last.astype(jnp.int32) + not_first.astype(jnp.int32))

    @pl.when(not_last)
    def _():
        relay_up.start()

    @pl.when(not_first)
    def _():
        relay_down.start()

    meta_plus[1].start()
    meta_minus[1].start()

    @pl.when(section == 0)
    def _():
        ring[0, 0] = outgoing[0]

    @pl.when(section == ns - 1)
    def _():
        ring[0, 1] = outgoing[1]

    def meta_step(j):
        for ways in (meta_plus, meta_minus):
            if j in ways:
                ways[j].wait_recv()
                if j + 1 in ways:
                    ways[j + 1].start()

    for j in range(1, LEAD + 1):
        meta_step(j)

    @pl.when(not_first)
    def _():
        relay_up.wait_recv()

    plus[0][1].start()
    minus[0][1].start()

    @pl.when(not_last)
    def _():
        relay_down.wait_recv()

    plus[1][1].start()
    minus[1][1].start()

    def spread_meta(k, rows, row_src):
        spread = jnp.zeros((rows, 128), F32)
        for s in range(PER_GROUP):
            spread = jnp.where(row_src == s, meta[k * PER_GROUP + s], spread)
        return spread

    def select(k):
        row, col = iota((64, 128), 0), iota((64, 128), 1)
        row_q, row_src, row_st, row_sl = row // 16, (row // 4) % 4, (row // 2) % 2, row % 2
        spread = spread_meta(k, 64, row_src)
        want = row_st * 8 + expert * CAP + row_sl
        tok = jnp.sum(jnp.where(col == want, spread, 0.0), axis=1, keepdims=True)
        target = (row_src * 32 + row_st * 16 + row_q * 4).astype(F32) + tok
        picker = jnp.where(col.astype(F32) == target, 1.0, 0.0).astype(BF16)
        rows = ring[k * PER_GROUP : (k + 1) * PER_GROUP].reshape(PER_GROUP * 2 * 16, q)
        picked = jnp.dot(picker, rows, preferred_element_type=F32)
        for i in range(QUARTERS):
            x[k, 0, :, i * q : (i + 1) * q] = picked[i * 16 : (i + 1) * 16].astype(BF16)

    def prepare_expand(k):
        row, col = iota((128, 128), 0), iota((128, 128), 1)
        row_src, row_st, row_q, row_t = row // 32, (row // 16) % 2, (row // 4) % 4, row % 4
        col_q, col_src = (col // 16) % 4, (col // 4) % 4
        col_st, col_sl = (col // 2) % 2, col % 2
        spread = spread_meta(k, 128, row_src)
        want = row_st * 8 + expert * CAP
        tok0 = jnp.sum(jnp.where(col == want, spread, 0.0), axis=1, keepdims=True)
        tok1 = jnp.sum(jnp.where(col == want + 1, spread, 0.0), axis=1, keepdims=True)
        tok = jnp.where(col_sl == 0, tok0, tok1)
        same = (row_q == col_q) & (row_src == col_src) & (row_st == col_st)
        expand[k] = jnp.where(same & (tok == row_t.astype(F32)), 1.0, 0.0).astype(BF16)
        row, col = iota((16, 128), 0), iota((16, 128), 1)
        spread = spread_meta(k, 16, row // 4)
        want = 16 + ((row // 2) % 2) * 8 + expert * CAP + row % 2
        gains = jnp.sum(jnp.where(col == want, spread, 0.0), axis=1, keepdims=True)
        gain_col[k] = jnp.broadcast_to(gains, (16, 128))

    def experts(k):
        hidden_in = jnp.dot(x[k].reshape(64, d), wgu[...], preferred_element_type=F32)
        gate, upper = hidden_in[:, :128], hidden_in[:, 128:]
        hidden = (gate * jax.nn.sigmoid(gate) * upper).astype(BF16)
        part = jnp.dot(hidden, wd[...], preferred_element_type=F32)
        p_own[k, 0] = part[0:16]
        p_send[k, 0] = part[16:32].astype(BF16)
        p_own[k, 1] = part[32:48]
        p_send[k, 1] = part[48:64].astype(BF16)
        p_twin[k].start()

    def unpack_weights(i, carry):
        rows = pl.ds(pl.multiple_of(i * 256, 256), 256)
        wgu[rows, :] = wgu_raw[rows].reshape(256, wgu.shape[1])
        return carry

    for j in range(1, half + 1):
        for s in range(2):
            for ways in (plus, minus):
                if j in ways[s]:
                    ways[s][j].wait_recv()
                    if j + 1 in ways[s]:
                        ways[s][j + 1].start()
        meta_step(j + LEAD)
        if j == 1:
            load_gu.wait()
            lax.fori_loop(0, d // 256, unpack_weights, 0)
            load_d.wait()
        if j % 2 == 0:
            k = j // 2 - 1
            select(k)
            x_across[k].start()
            x_twin[k].start()
            prepare_expand(k)
            if k > 0:
                x_across[k - 1].wait_recv()
                x_far[k - 1].start()
        elif j > 3:
            k = (j - 5) // 2
            x_twin[k].wait_recv()
            x_far[k].wait_recv()
            experts(k)

    last = groups - 1
    if groups > 1:
        x_twin[last - 1].wait_recv()
        x_far[last - 1].wait_recv()
        experts(last - 1)
    x_across[last].wait_recv()
    x_far[last].start()
    x_twin[last].wait_recv()
    x_far[last].wait_recv()
    experts(last)

    def sum_twins(k):
        p_twin[k].wait_recv()
        y_send[k] = (p_own[k, 1] + p_recv[k, 1].astype(F32)).astype(BF16)
        p_across[k].start()
        p_own[k, 0] = p_own[k, 0] + p_recv[k, 0].astype(F32)

    def to_tokens(k):
        p_across[k].wait_recv()
        total = (p_own[k, 0] + y_recv[k].astype(F32)) * gain_col[k][:, 0:1]
        stacked = jnp.concatenate([total[:, i * q : (i + 1) * q] for i in range(QUARTERS)], axis=0)
        high = stacked.astype(BF16)
        rest = (stacked - high.astype(F32)).astype(BF16)
        spread = jnp.dot(
            expand[k], jnp.concatenate([high, rest], axis=0), preferred_element_type=F32
        )
        contrib[k * PER_GROUP : (k + 1) * PER_GROUP] = spread.reshape(PER_GROUP, 2, 16, q)

    sum_twins(last)
    if groups > 1:
        sum_twins(last - 1)
    for j in range(1, half + 1):
        if j % 2 == 1:
            k = last - j // 2
            to_tokens(k)
            if k > 1:
                sum_twins(k - 2)
        distance = half + 1 - j
        for s in range(2):
            for way in range(2):
                if j in back[way][s]:
                    slot = nz - distance if way == 0 else distance
                    value = contrib[pos[slot % nz], s]
                    if j - 1 in back[way][s]:
                        back[way][s][j - 1].wait_recv()
                        value = value + rs_recv[way, j - 2, s].astype(F32)
                    rs_send[way, j - 1, s] = value.astype(BF16)
                    back[way][s][j].start()

    for s, out in enumerate((out_a, out_b)):
        value = ring[0, s].astype(F32) + contrib[0, s]
        for way in range(2):
            back[way][s][half].wait_recv()
            value = value + rs_recv[way, half - 1, s].astype(F32)
        for i in range(QUARTERS):
            out[:, i * q : (i + 1) * q] = value[i * TOK : (i + 1) * TOK].astype(BF16)

    @pl.when(not_last)
    def _():
        relay_up.wait_send()

    @pl.when(not_first)
    def _():
        relay_down.wait_send()

    every = list(meta_plus.values()) + list(meta_minus.values())
    for ways in (plus, minus, back[0], back[1]):
        every += list(ways[0].values()) + list(ways[1].values())
    for copy in every + x_across + x_twin + x_far + p_twin + p_across:
        copy.wait_send()


def shards(ns, nz, *args):
    tokens_a = args[0]
    d = tokens_a.shape[1]
    q = d // QUARTERS
    half, groups = nz // 2, nz // PER_GROUP
    width = args[7].shape[1]
    n = n_copies(nz)
    vmem = pl.BlockSpec(memory_space=pltpu.VMEM)
    smem = pl.BlockSpec(memory_space=pltpu.SMEM)
    hbm = pl.BlockSpec(memory_space=pl.ANY)
    return pl.pallas_call(
        functools.partial(kernel, ns, nz, d),
        out_shape=[jax.ShapeDtypeStruct(tokens_a.shape, BF16)] * 2,
        in_specs=[vmem] * 2 + [smem] * 4 + [hbm] * 2,
        out_specs=[vmem] * 2,
        scratch_shapes=[
            pltpu.VMEM((2, 16, q), BF16),
            pltpu.VMEM((nz, 2, 16, q), BF16),
            pltpu.VMEM((nz, 1, 128), F32),
            pltpu.VMEM((groups, 4, 16, d), BF16),
            pltpu.VMEM((d, 2, width), BF16),
            pltpu.VMEM((d, 2 * width), BF16),
            pltpu.VMEM((width, d), BF16),
            pltpu.VMEM((groups, 2, 16, d), F32),
            pltpu.VMEM((groups, 2, 16, d), BF16),
            pltpu.VMEM((groups, 2, 16, d), BF16),
            pltpu.VMEM((groups, 16, d), BF16),
            pltpu.VMEM((groups, 16, d), BF16),
            pltpu.VMEM((groups, 128, 128), BF16),
            pltpu.VMEM((groups, 16, 128), F32),
            pltpu.VMEM((nz, 2, 16, q), F32),
            pltpu.VMEM((2, half, 2, 16, q), BF16),
            pltpu.VMEM((2, half, 2, 16, q), BF16),
            pltpu.SemaphoreType.DMA((n,)),
            pltpu.SemaphoreType.DMA((n,)),
            pltpu.SemaphoreType.DMA((2,)),
        ],
        compiler_params=pltpu.CompilerParams(
            collective_id=0, has_side_effects=True, vmem_limit_bytes=60 * 1024 * 1024
        ),
    )(*args)


def solution(mesh):
    ns, nz = mesh.shape["section"], mesh.shape["ep"] // 4
    rows = P(("section", "ep"), None)
    in_specs = (rows,) * 6 + (P("section", None, None, "ep"), P("section", "ep", None))
    return jax.shard_map(
        functools.partial(shards, ns, nz),
        mesh=mesh,
        in_specs=in_specs,
        out_specs=(rows, rows),
        check_vma=False,
    )
```

```python
import functools

import jax
import jax.numpy as jnp
from jax import lax
from jax.experimental import pallas as pl
from jax.experimental.pallas import tpu as pltpu
from jax.sharding import PartitionSpec as P

EXPERTS = 4
TOP = 2
TOK = 4
CAP = 2
QUARTERS = 4
LINE = 4
NZ = EXPERTS * LINE
BF16 = jnp.bfloat16
F32 = jnp.float32
MESH = pl.DeviceIdType.MESH
N_SEMS = 80


def iota(shape, dim):
    return lax.broadcasted_iota(jnp.int32, shape, dim)


def find_tokens(routes, gains, stream, expert, slot):
    count = jnp.zeros(stream.shape, jnp.int32)
    token = jnp.zeros(stream.shape, jnp.int32)
    gain = jnp.zeros(stream.shape, F32)
    for t in range(TOK):
        for k in range(TOP):
            route = jnp.where(stream == 0, routes[0][k, t], routes[1][k, t])
            named = route == expert
            here = named & (count == slot)
            token = jnp.where(here, t, token)
            if gains is not None:
                value = jnp.where(stream == 0, gains[0][k, t], gains[1][k, t])
                gain = jnp.where(here, value, gain)
            count = count + named.astype(jnp.int32)
    return token, gain


def kernel(
    ns,
    d,
    tok_a,
    tok_b,
    routes_a,
    routes_b,
    gains_a,
    gains_b,
    wgu_hbm,
    wd_hbm,
    out_a,
    out_b,
    outgoing,
    current,
    packed,
    xin,
    wgu_raw,
    wgu,
    wd,
    gather,
    scatter,
    p_own,
    p_send,
    p_recv,
    y_send,
    y_recv,
    line_send,
    line_recv,
    opp_recv,
    far_send,
    far_recv,
    own_sum,
    send_sems,
    recv_sems,
    local_sems,
):
    q = d // QUARTERS
    section = lax.axis_index("section")
    ep = lax.axis_index("ep")
    z, low = ep // 4, ep % 4
    y, core = low // 2, low % 2
    g, i = z // LINE, z % LINE

    def at(to_z):
        return (section, to_z * 4 + low)

    plus4, minus4 = at((z + LINE) % NZ), at((z + NZ - LINE) % NZ)
    opp_first = LINE * ((g + 2) % EXPERTS)
    opp_rep = at(opp_first + jnp.where(i < 2, LINE - 1, 0))
    is_end = (i == 0) | (i == LINE - 1)
    served = jnp.where(i == 0, 2, 0)
    peers = [at(g * LINE + (i + m) % LINE) for m in range(1, LINE)]
    across = (section, ep + 2 - 4 * y)
    twin = (section, ep + 1 - 2 * core)
    up, down = (section + 1, ep), (section - 1, ep)
    not_last, not_first = section < ns - 1, section > 0

    load_gu = pltpu.make_async_copy(wgu_hbm.at[0], wgu_raw, local_sems.at[0])
    load_d = pltpu.make_async_copy(wd_hbm.at[0], wd, local_sems.at[1])

    barrier = pltpu.get_barrier_semaphore()

    def greet(device):
        pl.semaphore_signal(barrier, inc=1, device_id=device, device_id_type=MESH)

    greet(opp_rep)

    @pl.when(is_end)
    def _():
        greet(at(opp_first + served))
        greet(at(opp_first + served + 1))

    greet(plus4)
    greet(minus4)
    pl.when(not_last)(lambda: greet(up))
    pl.when(not_first)(lambda: greet(down))
    for peer in peers:
        greet(peer)
    greet(across)
    greet(twin)
    load_gu.start()
    load_d.start()

    used = [0]

    def sems(n=1):
        used[0] += n
        return used[0] - n

    def copy(src, dst, send_index, recv_index, device):
        return pltpu.make_async_remote_copy(
            src_ref=src,
            dst_ref=dst,
            send_sem=send_sems.at[send_index],
            recv_sem=recv_sems.at[recv_index],
            device_id=device,
            device_id_type=MESH,
        )

    def plain(src, dst, device):
        index = sems()
        return copy(src, dst, index, index, device)

    def arrived(dst, recv_index):
        copy(dst, dst, 0, recv_index, twin).wait_recv()

    for stream, tok in enumerate((tok_a, tok_b)):
        rows = tok[...].astype(F32)
        outgoing[stream] = jnp.concatenate(
            [rows[:, n * q : (n + 1) * q] for n in range(QUARTERS)], axis=0
        ).astype(BF16)

    relay_up = plain(outgoing.at[0], current.at[0], up)
    relay_down = plain(outgoing.at[1], current.at[1], down)

    pl.semaphore_wait(
        barrier,
        8
        + not_last.astype(jnp.int32)
        + not_first.astype(jnp.int32)
        + 2 * is_end.astype(jnp.int32),
    )
    pl.when(not_last)(relay_up.start)
    pl.when(not_first)(relay_down.start)

    @pl.when(section == 0)
    def _():
        current[0] = outgoing[0]

    @pl.when(section == ns - 1)
    def _():
        current[1] = outgoing[1]

    row, col = iota((64, 32), 0), iota((64, 32), 1)
    token, _ = find_tokens(
        (routes_a, routes_b), None, (row // 2) % 2, (g + row // 16) % EXPERTS, row % CAP
    )
    place = ((row // 2) % 2) * 16 + ((row // 4) % 4) * 4 + token
    picker = jnp.where(col == place, 1.0, 0.0).astype(BF16)

    lane = iota((1, 128), 1)
    token, gain = find_tokens(
        (routes_a, routes_b),
        (gains_a, gains_b),
        (lane // 2) % 2,
        (g + (lane // 16) % 4) % EXPERTS,
        lane % CAP,
    )
    high = gain.astype(BF16).astype(F32)
    weight = jnp.where(lane < 64, high, gain - high)
    row = iota((32, 128), 0)
    mine = (row % 4 == token) & ((row // 4) % 4 == (lane // 4) % 4) & (row // 16 == (lane // 2) % 2)
    mixing = jnp.where(mine, weight, 0.0).astype(BF16)

    row, col = iota((256, 256), 0), iota((256, 256), 1)
    place = ((row // 16) % 4) * 64 + ((row // 4) % 4) * 16 + (row // 64) * 4 + row % 4
    gather[...] = jnp.where(col == place, 1.0, 0.0).astype(BF16)
    row, col = iota((64, 64), 0), iota((64, 64), 1)
    place = ((row // 4) % 4) * 16 + (row // 16) * 4 + row % 4
    scatter[...] = jnp.where(col == place, 1.0, 0.0).astype(BF16)

    load_gu.wait()

    def unpack_weights(n, carry):
        rows = pl.ds(pl.multiple_of(n * 256, 256), 256)
        wgu[rows, :] = wgu_raw[rows].reshape(256, wgu.shape[1])
        return carry

    lax.fori_loop(0, d // 256, unpack_weights, 0)
    load_d.wait()

    pl.when(not_first)(relay_up.wait_recv)
    pl.when(not_last)(relay_down.wait_recv)

    picked = jnp.dot(picker, current[...].reshape(32, q), preferred_element_type=F32).astype(BF16)
    packed[0] = picked[32:48]
    far_sem, far_opp_recv = sems(), sems(2)
    far_opp = copy(
        packed.at[0], xin.at[0, 2 * LINE + i], far_sem, far_opp_recv + i % 2, opp_rep
    )
    far_opp.start()
    packed[1] = picked[16:32]
    packed[2] = picked[48:64]
    far_plus = plain(packed.at[1], xin.at[0, 3 * LINE + i], plus4)
    far_minus = plain(packed.at[2], xin.at[0, LINE + i], minus4)
    far_plus.start()
    far_minus.start()
    xin[0, i] = picked[0:16]

    started = [far_opp, far_plus, far_minus]

    line_sems = {}

    def line_out(o):
        line_sems[o] = sems(LINE - 1)
        for m in range(1, LINE):
            index = line_sems[o] + m - 1
            block = xin.at[0, o * LINE + i]
            out = copy(block, block, index, index, peers[m - 1])
            out.start()
            started.append(out)

    def line_in(o):
        for m in range(1, LINE):
            arrived(xin.at[0, o * LINE + (i + LINE - m) % LINE], line_sems[o] + m - 1)

    x_across, x_twin, x_far, p_twin, p_across = {}, {}, {}, {}, {}
    for o in range(EXPERTS):
        block = pl.ds(o * LINE, LINE)
        x_across[o] = plain(xin.at[0, block], xin.at[2, block], across)
        x_twin[o] = plain(xin.at[0, block], xin.at[1, block], twin)
        x_far[o] = plain(xin.at[2, block], xin.at[3, block], twin)
        p_twin[o] = plain(p_send.at[o], p_recv.at[o], twin)
        p_across[o] = plain(y_send.at[o], y_recv.at[o], across)
    for group in (x_across, x_twin, x_far, p_twin, p_across):
        started += list(group.values())

    def share(o):
        x_across[o].start()
        x_twin[o].start()

    def pass_on(o):
        x_across[o].wait_recv()
        x_far[o].start()

    def experts(o):
        x_twin[o].wait_recv()
        x_far[o].wait_recv()
        rows = xin[:, o * LINE : (o + 1) * LINE].reshape(256, q)
        sorted_rows = jnp.dot(gather[...], rows, preferred_element_type=F32).astype(BF16)
        projected = jnp.zeros((64, wgu.shape[1]), F32)
        for n in range(QUARTERS):
            projected += jnp.dot(
                sorted_rows[n * 64 : (n + 1) * 64],
                wgu[n * q : (n + 1) * q],
                preferred_element_type=F32,
            )
        gate, upper = projected[:, :128], projected[:, 128:]
        hidden = (gate * jax.nn.sigmoid(gate) * upper).astype(BF16)
        part = jnp.dot(hidden, wd[...], preferred_element_type=F32)
        p_send[o, 0] = part[16:32].astype(BF16)
        p_send[o, 1] = part[48:64].astype(BF16)
        p_twin[o].start()
        p_own[o, 0] = part[0:16]
        p_own[o, 1] = part[32:48]

    def sum_twins(o):
        p_twin[o].wait_recv()
        y_send[o] = (p_own[o, 1] + p_recv[o, 1].astype(F32)).astype(BF16)
        p_across[o].start()
        p_own[o, 0] = p_own[o, 0] + p_recv[o, 0].astype(F32)

    def to_blocks(o):
        p_across[o].wait_recv()
        total = (p_own[o, 0] + y_recv[o].astype(F32)).astype(BF16)
        stacked = jnp.concatenate([total[:, n * q : (n + 1) * q] for n in range(QUARTERS)], axis=0)
        blocks = jnp.dot(scatter[...], stacked, preferred_element_type=F32).astype(BF16)
        line_send[o] = blocks.reshape(LINE, 16, q)

    back_sems = {}

    def line_back(o):
        back_sems[o] = sems(LINE - 1)
        for m in range(1, LINE):
            index = back_sems[o] + m - 1
            out = copy(
                line_send.at[o, (i + m) % LINE], line_recv.at[o, m - 1], index, index, peers[m - 1]
            )
            out.start()
            started.append(out)

    def line_sum(o):
        total = line_send[o, i].astype(F32)
        for m in range(1, LINE):
            arrived(line_recv.at[o, m - 1], back_sems[o] + m - 1)
            total = total + line_recv[o, m - 1].astype(F32)
        return total.astype(BF16)

    line_out(0)
    line_in(0)
    share(0)
    far_minus.wait_recv()
    line_out(1)
    far_plus.wait_recv()
    line_out(3)

    opp_send, opp_from = sems(LINE - 1), sems(2)
    half_block = xin.at[0, pl.ds(2 * LINE + served, 2)]
    opp_line = [
        copy(half_block, half_block, opp_send + m, opp_from + jnp.where(i == 0, 0, 1), peers[m])
        for m in range(LINE - 1)
    ]

    @pl.when(is_end)
    def _():
        arrived(xin.at[0, 2 * LINE + served], far_opp_recv)
        arrived(xin.at[0, 2 * LINE + served + 1], far_opp_recv + 1)
        for out in opp_line:
            out.start()

    pass_on(0)
    experts(0)
    line_in(1)
    share(1)
    line_in(3)
    share(3)

    @pl.when(i != 0)
    def _():
        arrived(xin.at[0, pl.ds(2 * LINE + 2, 2)], opp_from)

    @pl.when(i != LINE - 1)
    def _():
        arrived(xin.at[0, pl.ds(2 * LINE, 2)], opp_from + 1)

    share(2)
    sum_twins(0)
    pass_on(1)
    experts(1)
    pass_on(3)
    experts(3)
    to_blocks(0)
    line_back(0)
    sum_twins(1)
    sum_twins(3)
    pass_on(2)
    experts(2)
    sum_twins(2)
    to_blocks(1)
    line_back(1)
    to_blocks(3)
    line_back(3)
    to_blocks(2)

    opp_back, opp_back_recv = sems(2), sems(LINE - 1)
    away0, away3 = (LINE - i) % LINE, LINE - 1 - i
    to_first = copy(
        line_send.at[2, pl.ds(2, 2)],
        opp_recv.at[jnp.maximum(away0 - 1, 0)],
        opp_back,
        opp_back_recv + jnp.maximum(away0 - 1, 0),
        at(g * LINE),
    )
    to_final = copy(
        line_send.at[2, pl.ds(0, 2)],
        opp_recv.at[jnp.maximum(away3 - 1, 0)],
        opp_back + 1,
        opp_back_recv + jnp.maximum(away3 - 1, 0),
        at(g * LINE + LINE - 1),
    )
    pl.when(i != 0)(to_first.start)
    pl.when(i != LINE - 1)(to_final.start)

    far_send[0] = line_sum(1)
    return_plus = plain(far_send.at[0], far_recv.at[2], plus4)
    return_plus.start()
    far_send[1] = line_sum(3)
    return_minus = plain(far_send.at[1], far_recv.at[0], minus4)
    return_minus.start()
    started += [return_plus, return_minus]

    return_opp, return_opp_recv = sems(2), sems()
    returns = [
        copy(
            far_send.at[2 + n],
            far_recv.at[1],
            return_opp + n,
            return_opp_recv,
            at(opp_first + served + n),
        )
        for n in range(2)
    ]

    @pl.when(is_end)
    def _():
        total = line_send[2, pl.ds(served, 2)].astype(F32)
        for m in range(LINE - 1):
            arrived(opp_recv.at[m], opp_back_recv + m)
            total = total + opp_recv[m].astype(F32)
        far_send[2:4] = total.astype(BF16)
        for out in returns:
            out.start()

    own_sum[...] = line_sum(0)

    pl.when(not_last)(relay_up.wait_send)
    pl.when(not_first)(relay_down.wait_send)
    for out in started:
        out.wait_send()

    @pl.when(is_end)
    def _():
        for out in opp_line + returns:
            out.wait_send()

    pl.when(i != 0)(to_first.wait_send)
    pl.when(i != LINE - 1)(to_final.wait_send)

    return_plus.wait_recv()
    return_minus.wait_recv()
    arrived(far_recv.at[1], return_opp_recv)
    parts = jnp.concatenate([own_sum[...]] + [far_recv[n] for n in range(3)], axis=0)
    added = jnp.dot(mixing, jnp.concatenate([parts, parts], axis=0), preferred_element_type=F32)
    mixed = current[...].reshape(32, q).astype(F32) + added
    for s, out in enumerate((out_a, out_b)):
        for n in range(QUARTERS):
            first = s * 16 + n * TOK
            out[:, n * q : (n + 1) * q] = mixed[first : first + TOK].astype(BF16)


def shards(ns, *args):
    tokens_a = args[0]
    d = tokens_a.shape[1]
    q = d // QUARTERS
    width = args[7].shape[1]
    vmem = pl.BlockSpec(memory_space=pltpu.VMEM)
    smem = pl.BlockSpec(memory_space=pltpu.SMEM)
    hbm = pl.BlockSpec(memory_space=pl.ANY)
    small = [array.T for array in args[2:6]]
    return pl.pallas_call(
        functools.partial(kernel, ns, d),
        out_shape=[jax.ShapeDtypeStruct(tokens_a.shape, BF16)] * 2,
        in_specs=[vmem] * 2 + [smem] * 4 + [hbm] * 2,
        out_specs=[vmem] * 2,
        scratch_shapes=[
            pltpu.VMEM((2, 16, q), BF16),
            pltpu.VMEM((2, 16, q), BF16),
            pltpu.VMEM((3, 16, q), BF16),
            pltpu.VMEM((4, NZ, 16, q), BF16),
            pltpu.VMEM((d, 2, width), BF16),
            pltpu.VMEM((d, 2 * width), BF16),
            pltpu.VMEM((width, d), BF16),
            pltpu.VMEM((256, 256), BF16),
            pltpu.VMEM((64, 64), BF16),
            pltpu.VMEM((EXPERTS, 2, 16, d), F32),
            pltpu.VMEM((EXPERTS, 2, 16, d), BF16),
            pltpu.VMEM((EXPERTS, 2, 16, d), BF16),
            pltpu.VMEM((EXPERTS, 16, d), BF16),
            pltpu.VMEM((EXPERTS, 16, d), BF16),
            pltpu.VMEM((EXPERTS, LINE, 16, q), BF16),
            pltpu.VMEM((EXPERTS, LINE - 1, 16, q), BF16),
            pltpu.VMEM((LINE - 1, 2, 16, q), BF16),
            pltpu.VMEM((4, 16, q), BF16),
            pltpu.VMEM((3, 16, q), BF16),
            pltpu.VMEM((16, q), BF16),
            pltpu.SemaphoreType.DMA((N_SEMS,)),
            pltpu.SemaphoreType.DMA((N_SEMS,)),
            pltpu.SemaphoreType.DMA((2,)),
        ],
        compiler_params=pltpu.CompilerParams(
            collective_id=0, has_side_effects=True, vmem_limit_bytes=60 * 1024 * 1024
        ),
    )(*args[:2], *small, *args[6:])


def solution(mesh):
    ns = mesh.shape["section"]
    rows = P(("section", "ep"), None)
    in_specs = (rows,) * 6 + (P("section", None, None, "ep"), P("section", "ep", None))
    return jax.shard_map(
        functools.partial(shards, ns),
        mesh=mesh,
        in_specs=in_specs,
        out_specs=(rows, rows),
        check_vma=False,
    )
```

```python
import functools

import jax
import jax.numpy as jnp
from jax import lax
from jax.experimental import pallas as pl
from jax.experimental.pallas import tpu as pltpu
from jax.sharding import PartitionSpec as P

EXPERTS = 4
TOP = 2
TOK = 4
CAP = 2
QUARTERS = 4
LINE = 4
NZ = EXPERTS * LINE
BF16 = jnp.bfloat16
F32 = jnp.float32
MESH = pl.DeviceIdType.MESH
N_SEMS = 80


def iota(shape, dim):
    return lax.broadcasted_iota(jnp.int32, shape, dim)


def find_tokens(routes, gains, stream, expert, slot):
    count = jnp.zeros(stream.shape, jnp.int32)
    token = jnp.zeros(stream.shape, jnp.int32)
    gain = jnp.zeros(stream.shape, F32)
    for t in range(TOK):
        for k in range(TOP):
            route = jnp.where(stream == 0, routes[0][k, t], routes[1][k, t])
            named = route == expert
            here = named & (count == slot)
            token = jnp.where(here, t, token)
            if gains is not None:
                value = jnp.where(stream == 0, gains[0][k, t], gains[1][k, t])
                gain = jnp.where(here, value, gain)
            count = count + named.astype(jnp.int32)
    return token, gain


def kernel(
    ns,
    d,
    tok_a,
    tok_b,
    routes_a,
    routes_b,
    gains_a,
    gains_b,
    wgu_hbm,
    wd_hbm,
    out_a,
    out_b,
    outgoing,
    current,
    packed,
    xin,
    wgu_raw,
    wgu,
    wd,
    gather,
    scatter,
    p_own,
    p_send,
    p_recv,
    y_send,
    y_recv,
    line_send,
    line_recv,
    far_send,
    far_recv,
    own_sum,
    send_sems,
    recv_sems,
    local_sems,
    met,
):
    q = d // QUARTERS
    section = lax.axis_index("section")
    ep = lax.axis_index("ep")
    z, low = ep // 4, ep % 4
    y, core = low // 2, low % 2
    g, i = z // LINE, z % LINE

    def at(to_z):
        return (section, to_z * 4 + low)

    plus4, minus4 = at((z + LINE) % NZ), at((z + NZ - LINE) % NZ)
    opposite_z = LINE * ((g + 2) % EXPERTS) + LINE - 1 - i
    opposite = at(opposite_z)
    peers = [at(g * LINE + (i + m) % LINE) for m in range(1, LINE)]
    across = (section, ep + 2 - 4 * y)
    twin = (section, ep + 1 - 2 * core)
    up, down = (section + 1, ep), (section - 1, ep)
    not_last, not_first = section < ns - 1, section > 0

    load_gu = pltpu.make_async_copy(wgu_hbm.at[0], wgu_raw, local_sems.at[0])
    load_d = pltpu.make_async_copy(wd_hbm.at[0], wd, local_sems.at[1])

    barrier = pltpu.get_barrier_semaphore()

    def signal(semaphore, device):
        pl.semaphore_signal(semaphore, inc=1, device_id=device, device_id_type=MESH)

    def greet(to_section, to_z, to_y, to_core):
        signal(barrier, (to_section, to_z * 4 + to_y * 2 + to_core))

    greet(section, opposite_z, y, 1)
    greet(section, (z + LINE) % NZ, y, 1)
    greet(section, (z + NZ - LINE) % NZ, y, 1)
    pl.when(not_last)(lambda: greet(section + 1, z, y, 0))
    pl.when(not_first)(lambda: greet(section - 1, z, y, 0))
    for m in range(1, LINE):
        greet(section, g * LINE + (i + m) % LINE, y, 0)
    greet(section, z, 1 - y, 0)
    signal(barrier, twin)
    load_gu.start()
    load_d.start()

    used = [0]

    def sems(n=1):
        used[0] += n
        return used[0] - n

    def copy(src, dst, send_index, recv_index, device):
        return pltpu.make_async_remote_copy(
            src_ref=src,
            dst_ref=dst,
            send_sem=send_sems.at[send_index],
            recv_sem=recv_sems.at[recv_index],
            device_id=device,
            device_id_type=MESH,
        )

    def plain(src, dst, device):
        index = sems()
        return copy(src, dst, index, index, device)

    def arrived(dst, recv_index):
        copy(dst, dst, 0, recv_index, twin).wait_recv()

    for stream, tok in enumerate((tok_a, tok_b)):
        rows = tok[...].astype(F32)
        outgoing[stream] = jnp.concatenate(
            [rows[:, n * q : (n + 1) * q] for n in range(QUARTERS)], axis=0
        ).astype(BF16)

    relay_up = plain(outgoing.at[0], current.at[0], up)
    relay_down = plain(outgoing.at[1], current.at[1], down)

    near = 2 * (LINE + not_last.astype(jnp.int32) + not_first.astype(jnp.int32)) + 1
    far = 2 * 3 + 1

    @pl.when(core == 0)
    def _():
        pl.semaphore_wait(barrier, near)
        signal(met, twin)

    @pl.when(core == 1)
    def _():
        pl.semaphore_wait(met, 1)

    pl.when(not_last)(relay_up.start)
    pl.when(not_first)(relay_down.start)

    @pl.when(section == 0)
    def _():
        current[0] = outgoing[0]

    @pl.when(section == ns - 1)
    def _():
        current[1] = outgoing[1]

    row, col = iota((64, 32), 0), iota((64, 32), 1)
    token, _ = find_tokens(
        (routes_a, routes_b), None, (row // 2) % 2, (g + row // 16) % EXPERTS, row % CAP
    )
    place = ((row // 2) % 2) * 16 + ((row // 4) % 4) * 4 + token
    picker = jnp.where(col == place, 1.0, 0.0).astype(BF16)

    lane = iota((1, 128), 1)
    token, gain = find_tokens(
        (routes_a, routes_b),
        (gains_a, gains_b),
        (lane // 2) % 2,
        (g + (lane // 16) % 4) % EXPERTS,
        lane % CAP,
    )
    high = gain.astype(BF16).astype(F32)
    weight = jnp.where(lane < 64, high, gain - high)
    row = iota((32, 128), 0)
    mine = (row % 4 == token) & ((row // 4) % 4 == (lane // 4) % 4) & (row // 16 == (lane // 2) % 2)
    mixing = jnp.where(mine, weight, 0.0).astype(BF16)

    row, col = iota((256, 256), 0), iota((256, 256), 1)
    place = ((row // 16) % 4) * 64 + ((row // 4) % 4) * 16 + (row // 64) * 4 + row % 4
    gather[...] = jnp.where(col == place, 1.0, 0.0).astype(BF16)
    row, col = iota((64, 64), 0), iota((64, 64), 1)
    place = ((row // 4) % 4) * 16 + (row // 16) * 4 + row % 4
    scatter[...] = jnp.where(col == place, 1.0, 0.0).astype(BF16)

    load_gu.wait()

    def unpack_weights(n, carry):
        rows = pl.ds(pl.multiple_of(n * 256, 256), 256)
        wgu[rows, :] = wgu_raw[rows].reshape(256, wgu.shape[1])
        return carry

    lax.fori_loop(0, d // 256, unpack_weights, 0)
    load_d.wait()

    pl.when(not_first)(relay_up.wait_recv)
    pl.when(not_last)(relay_down.wait_recv)

    picked = jnp.dot(picker, current[...].reshape(32, q), preferred_element_type=F32).astype(BF16)
    xin[0, i] = picked[0:16]
    packed[0] = picked[32:48]
    packed[1] = picked[16:32]
    packed[2] = picked[48:64]
    far_opp = plain(packed.at[0], xin.at[0, 2 * LINE + i], opposite)
    far_plus = plain(packed.at[1], xin.at[0, 3 * LINE + i], plus4)
    far_minus = plain(packed.at[2], xin.at[0, LINE + i], minus4)
    started = [far_opp, far_plus, far_minus]

    def held(o, j):
        return 2 * LINE + LINE - 1 - j if o == 2 else o * LINE + j

    x_across, x_twin, x_far, p_twin, p_across, line_sems = {}, {}, {}, {}, {}, {}
    for o in range(EXPERTS):
        block = pl.ds(o * LINE, LINE)
        x_across[o] = []
        for m in range(LINE):
            place = held(o, (i + LINE - m) % LINE)
            x_across[o].append(plain(xin.at[0, place], xin.at[2, place], across))
        x_twin[o] = plain(xin.at[0, block], xin.at[1, block], twin)
        x_far[o] = plain(xin.at[2, block], xin.at[3, block], twin)
        p_twin[o] = plain(p_send.at[o], p_recv.at[o], twin)
        p_across[o] = plain(y_send.at[o], y_recv.at[o], across)
        started += x_across[o] + [x_twin[o], x_far[o], p_twin[o], p_across[o]]

    def line_out(o):
        line_sems[o] = sems(LINE - 1)
        for m in range(1, LINE):
            index = line_sems[o] + m - 1
            block = xin.at[0, held(o, i)]
            out = copy(block, block, index, index, peers[m - 1])
            out.start()
            started.append(out)
        x_across[o][0].start()

    def line_in(o):
        for m in range(1, LINE):
            arrived(xin.at[0, held(o, (i + LINE - m) % LINE)], line_sems[o] + m - 1)
            x_across[o][m].start()
        x_twin[o].start()

    def pass_on(o):
        for part in x_across[o]:
            part.wait_recv()
        x_far[o].start()

    def experts(o):
        x_twin[o].wait_recv()
        x_far[o].wait_recv()
        rows = xin[:, o * LINE : (o + 1) * LINE].reshape(256, q)
        sorted_rows = jnp.dot(gather[...], rows, preferred_element_type=F32).astype(BF16)
        projected = jnp.zeros((64, wgu.shape[1]), F32)
        for n in range(QUARTERS):
            projected += jnp.dot(
                sorted_rows[n * 64 : (n + 1) * 64],
                wgu[n * q : (n + 1) * q],
                preferred_element_type=F32,
            )
        gate, upper = projected[:, :128], projected[:, 128:]
        hidden = (gate * jax.nn.sigmoid(gate) * upper).astype(BF16)
        part = jnp.dot(hidden, wd[...], preferred_element_type=F32)
        p_send[o, 0] = part[16:32].astype(BF16)
        p_send[o, 1] = part[48:64].astype(BF16)
        p_twin[o].start()
        p_own[o, 0] = part[0:16]
        p_own[o, 1] = part[32:48]

    def sum_twins(o):
        p_twin[o].wait_recv()
        y_send[o] = (p_own[o, 1] + p_recv[o, 1].astype(F32)).astype(BF16)
        p_across[o].start()
        p_own[o, 0] = p_own[o, 0] + p_recv[o, 0].astype(F32)

    def to_blocks(o):
        p_across[o].wait_recv()
        total = (p_own[o, 0] + y_recv[o].astype(F32)).astype(BF16)
        stacked = jnp.concatenate([total[:, n * q : (n + 1) * q] for n in range(QUARTERS)], axis=0)
        blocks = jnp.dot(scatter[...], stacked, preferred_element_type=F32).astype(BF16)
        line_send[o] = blocks.reshape(LINE, 16, q)

    back_sems = {}

    def line_back(o):
        back_sems[o] = sems(LINE - 1)
        for m in range(1, LINE):
            index = back_sems[o] + m - 1
            block = held(o, (i + m) % LINE) - o * LINE
            out = copy(line_send.at[o, block], line_recv.at[o, m - 1], index, index, peers[m - 1])
            out.start()
            started.append(out)

    def line_sum(o):
        total = line_send[o, held(o, i) - o * LINE].astype(F32)
        for m in range(1, LINE):
            arrived(line_recv.at[o, m - 1], back_sems[o] + m - 1)
            total = total + line_recv[o, m - 1].astype(F32)
        return total.astype(BF16)

    line_out(0)

    @pl.when(core == 1)
    def _():
        pl.semaphore_wait(barrier, far)
        signal(met, twin)

    @pl.when(core == 0)
    def _():
        pl.semaphore_wait(met, 1)

    far_opp.start()
    far_plus.start()
    far_minus.start()
    line_in(0)
    far_minus.wait_recv()
    line_out(1)
    far_plus.wait_recv()
    line_out(3)
    far_opp.wait_recv()
    line_out(2)
    pass_on(0)
    experts(0)
    line_in(1)
    line_in(3)
    line_in(2)
    sum_twins(0)
    pass_on(1)
    experts(1)
    pass_on(3)
    experts(3)
    to_blocks(0)
    line_back(0)
    sum_twins(1)
    sum_twins(3)
    pass_on(2)
    experts(2)
    sum_twins(2)
    to_blocks(1)
    line_back(1)
    to_blocks(3)
    line_back(3)
    to_blocks(2)
    line_back(2)

    returns = []
    for o, slot, device in ((1, 2, plus4), (3, 0, minus4), (2, 1, opposite)):
        far_send[o - 1] = line_sum(o)
        returns.append(plain(far_send.at[o - 1], far_recv.at[slot], device))
        returns[-1].start()
    started += returns

    own_sum[...] = line_sum(0)

    pl.when(not_last)(relay_up.wait_send)
    pl.when(not_first)(relay_down.wait_send)
    for out in started:
        out.wait_send()

    for out in returns:
        out.wait_recv()
    parts = jnp.concatenate([own_sum[...]] + [far_recv[n] for n in range(3)], axis=0)
    added = jnp.dot(mixing, jnp.concatenate([parts, parts], axis=0), preferred_element_type=F32)
    mixed = current[...].reshape(32, q).astype(F32) + added
    for s, out in enumerate((out_a, out_b)):
        for n in range(QUARTERS):
            first = s * 16 + n * TOK
            out[:, n * q : (n + 1) * q] = mixed[first : first + TOK].astype(BF16)


def shards(ns, *args):
    tokens_a = args[0]
    d = tokens_a.shape[1]
    q = d // QUARTERS
    width = args[7].shape[1]
    vmem = pl.BlockSpec(memory_space=pltpu.VMEM)
    smem = pl.BlockSpec(memory_space=pltpu.SMEM)
    hbm = pl.BlockSpec(memory_space=pl.ANY)
    small = [array.T for array in args[2:6]]
    return pl.pallas_call(
        functools.partial(kernel, ns, d),
        out_shape=[jax.ShapeDtypeStruct(tokens_a.shape, BF16)] * 2,
        in_specs=[vmem] * 2 + [smem] * 4 + [hbm] * 2,
        out_specs=[vmem] * 2,
        scratch_shapes=[
            pltpu.VMEM((2, 16, q), BF16),
            pltpu.VMEM((2, 16, q), BF16),
            pltpu.VMEM((3, 16, q), BF16),
            pltpu.VMEM((4, NZ, 16, q), BF16),
            pltpu.VMEM((d, 2, width), BF16),
            pltpu.VMEM((d, 2 * width), BF16),
            pltpu.VMEM((width, d), BF16),
            pltpu.VMEM((256, 256), BF16),
            pltpu.VMEM((64, 64), BF16),
            pltpu.VMEM((EXPERTS, 2, 16, d), F32),
            pltpu.VMEM((EXPERTS, 2, 16, d), BF16),
            pltpu.VMEM((EXPERTS, 2, 16, d), BF16),
            pltpu.VMEM((EXPERTS, 16, d), BF16),
            pltpu.VMEM((EXPERTS, 16, d), BF16),
            pltpu.VMEM((EXPERTS, LINE, 16, q), BF16),
            pltpu.VMEM((EXPERTS, LINE - 1, 16, q), BF16),
            pltpu.VMEM((3, 16, q), BF16),
            pltpu.VMEM((3, 16, q), BF16),
            pltpu.VMEM((16, q), BF16),
            pltpu.SemaphoreType.DMA((N_SEMS,)),
            pltpu.SemaphoreType.DMA((N_SEMS,)),
            pltpu.SemaphoreType.DMA((2,)),
            pltpu.SemaphoreType.REGULAR,
        ],
        compiler_params=pltpu.CompilerParams(
            collective_id=0, has_side_effects=True, vmem_limit_bytes=60 * 1024 * 1024
        ),
    )(*args[:2], *small, *args[6:])


def solution(mesh):
    ns = mesh.shape["section"]
    rows = P(("section", "ep"), None)
    in_specs = (rows,) * 6 + (P("section", None, None, "ep"), P("section", "ep", None))
    return jax.shard_map(
        functools.partial(shards, ns),
        mesh=mesh,
        in_specs=in_specs,
        out_specs=(rows, rows),
        check_vma=False,
    )
```

```python
import functools

import jax
import jax.numpy as jnp
from jax import lax
from jax.experimental import pallas as pl
from jax.experimental.pallas import tpu as pltpu
from jax.sharding import PartitionSpec as P

EXPERTS = 4
TOP = 2
TOK = 4
CAP = 2
QUARTERS = 4
LINE = 4
NZ = EXPERTS * LINE
BF16 = jnp.bfloat16
F32 = jnp.float32
MESH = pl.DeviceIdType.MESH
N_SEMS = 80


def iota(shape, dim):
    return lax.broadcasted_iota(jnp.int32, shape, dim)


def find_tokens(routes, gains, stream, expert, slot):
    count = jnp.zeros(stream.shape, jnp.int32)
    token = jnp.zeros(stream.shape, jnp.int32)
    gain = jnp.zeros(stream.shape, F32)
    for t in range(TOK):
        for k in range(TOP):
            route = jnp.where(stream == 0, routes[0][k, t], routes[1][k, t])
            named = route == expert
            here = named & (count == slot)
            token = jnp.where(here, t, token)
            if gains is not None:
                value = jnp.where(stream == 0, gains[0][k, t], gains[1][k, t])
                gain = jnp.where(here, value, gain)
            count = count + named.astype(jnp.int32)
    return token, gain


def kernel(
    ns,
    d,
    tok_a,
    tok_b,
    routes_a,
    routes_b,
    gains_a,
    gains_b,
    wgu_hbm,
    wd_hbm,
    result,
    outgoing,
    current,
    packed,
    xin,
    wgu_raw,
    wgu,
    wd,
    gather,
    scatter,
    p_own,
    p_send,
    p_recv,
    y_send,
    y_recv,
    line_send,
    line_recv,
    far_send,
    far_recv,
    own_sum,
    send_sems,
    recv_sems,
    local_sems,
    met,
):
    q = d // QUARTERS
    section = lax.axis_index("section")
    ep = lax.axis_index("ep")
    z, low = ep // 4, ep % 4
    y, core = low // 2, low % 2
    g, i = z // LINE, z % LINE

    def at(to_z):
        return (section, to_z * 4 + low)

    plus4, minus4 = at((z + LINE) % NZ), at((z + NZ - LINE) % NZ)
    opposite_z = LINE * ((g + 2) % EXPERTS) + LINE - 1 - i
    opposite = at(opposite_z)
    peers = [at(g * LINE + (i + m) % LINE) for m in range(1, LINE)]
    across = (section, ep + 2 - 4 * y)
    twin = (section, ep + 1 - 2 * core)
    up, down = (section + 1, ep), (section - 1, ep)
    not_last, not_first = section < ns - 1, section > 0

    load_gu = pltpu.make_async_copy(wgu_hbm.at[0], wgu_raw, local_sems.at[0])
    load_d = pltpu.make_async_copy(wd_hbm.at[0], wd, local_sems.at[1])

    barrier = pltpu.get_barrier_semaphore()

    def signal(semaphore, device):
        pl.semaphore_signal(semaphore, inc=1, device_id=device, device_id_type=MESH)

    def greet(to_section, to_z, to_y, to_core):
        signal(barrier, (to_section, to_z * 4 + to_y * 2 + to_core))

    greet(section, opposite_z, y, 1)
    greet(section, (z + LINE) % NZ, y, 1)
    greet(section, (z + NZ - LINE) % NZ, y, 1)
    pl.when(not_last)(lambda: greet(section + 1, z, y, 0))
    pl.when(not_first)(lambda: greet(section - 1, z, y, 0))
    for m in range(1, LINE):
        greet(section, g * LINE + (i + m) % LINE, y, 0)
    greet(section, z, 1 - y, 0)
    signal(barrier, twin)
    load_gu.start()
    load_d.start()

    used = [0]

    def sems(n=1):
        used[0] += n
        return used[0] - n

    def copy(src, dst, send_index, recv_index, device):
        return pltpu.make_async_remote_copy(
            src_ref=src,
            dst_ref=dst,
            send_sem=send_sems.at[send_index],
            recv_sem=recv_sems.at[recv_index],
            device_id=device,
            device_id_type=MESH,
        )

    def plain(src, dst, device):
        index = sems()
        return copy(src, dst, index, index, device)

    def arrived(dst, recv_index):
        copy(dst, dst, 0, recv_index, twin).wait_recv()

    for stream, tok in enumerate((tok_a, tok_b)):
        rows = tok[...].astype(F32)
        outgoing[stream] = jnp.concatenate(
            [rows[:, n * q : (n + 1) * q] for n in range(QUARTERS)], axis=0
        ).astype(BF16)

    relay_up = plain(outgoing.at[0], current.at[0], up)
    relay_down = plain(outgoing.at[1], current.at[1], down)

    near = 2 * (LINE + not_last.astype(jnp.int32) + not_first.astype(jnp.int32)) + 1
    far = 2 * 3 + 1

    @pl.when(core == 0)
    def _():
        pl.semaphore_wait(barrier, near)
        signal(met, twin)

    @pl.when(core == 1)
    def _():
        pl.semaphore_wait(met, 1)

    pl.when(not_last)(relay_up.start)
    pl.when(not_first)(relay_down.start)

    @pl.when(section == 0)
    def _():
        current[0] = outgoing[0]

    @pl.when(section == ns - 1)
    def _():
        current[1] = outgoing[1]

    row, col = iota((64, 32), 0), iota((64, 32), 1)
    token, _ = find_tokens(
        (routes_a, routes_b), None, (row // 2) % 2, (g + row // 16) % EXPERTS, row % CAP
    )
    place = ((row // 2) % 2) * 16 + ((row // 4) % 4) * 4 + token
    picker = jnp.where(col == place, 1.0, 0.0).astype(BF16)

    lane = iota((1, 128), 1)
    token, gain = find_tokens(
        (routes_a, routes_b),
        (gains_a, gains_b),
        (lane // 2) % 2,
        (g + (lane // 16) % 4) % EXPERTS,
        lane % CAP,
    )
    high = gain.astype(BF16).astype(F32)
    weight = jnp.where(lane < 64, high, gain - high)
    row = iota((32, 128), 0)
    mine = (row % 4 == token) & ((row // 4) % 4 == (lane // 4) % 4) & (row // 16 == (lane // 2) % 2)
    mixing = jnp.where(mine, weight, 0.0).astype(BF16)

    row, col = iota((256, 256), 0), iota((256, 256), 1)
    place = ((row // 16) % 4) * 64 + ((row // 4) % 4) * 16 + (row // 64) * 4 + row % 4
    gather[...] = jnp.where(col == place, 1.0, 0.0).astype(BF16)
    row, col = iota((64, 64), 0), iota((64, 64), 1)
    place = ((row // 4) % 4) * 16 + (row // 16) * 4 + row % 4
    scatter[...] = jnp.where(col == place, 1.0, 0.0).astype(BF16)

    load_gu.wait()

    def unpack_weights(n, carry):
        rows = pl.ds(pl.multiple_of(n * 256, 256), 256)
        wgu[rows, :] = wgu_raw[rows].reshape(256, wgu.shape[1])
        return carry

    lax.fori_loop(0, d // 256, unpack_weights, 0)
    load_d.wait()

    pl.when(not_first)(relay_up.wait_recv)
    pl.when(not_last)(relay_down.wait_recv)

    picked = jnp.dot(picker, current[...].reshape(32, q), preferred_element_type=F32).astype(BF16)
    xin[0, i] = picked[0:16]
    packed[0] = picked[32:48]
    packed[1] = picked[16:32]
    packed[2] = picked[48:64]
    far_opp = plain(packed.at[0], xin.at[0, 2 * LINE + i], opposite)
    far_plus = plain(packed.at[1], xin.at[0, 3 * LINE + i], plus4)
    far_minus = plain(packed.at[2], xin.at[0, LINE + i], minus4)
    started = [far_opp, far_plus, far_minus]

    def held(o, j):
        return 2 * LINE + LINE - 1 - j if o == 2 else o * LINE + j

    x_across, x_twin, x_far, p_twin, p_across, line_sems = {}, {}, {}, {}, {}, {}
    for o in range(EXPERTS):
        block = pl.ds(o * LINE, LINE)
        x_across[o] = []
        for m in range(LINE):
            place = held(o, (i + LINE - m) % LINE)
            x_across[o].append(plain(xin.at[0, place], xin.at[2, place], across))
        x_twin[o] = plain(xin.at[0, block], xin.at[1, block], twin)
        x_far[o] = plain(xin.at[2, block], xin.at[3, block], twin)
        p_twin[o] = plain(p_send.at[o], p_recv.at[o], twin)
        p_across[o] = plain(y_send.at[o], y_recv.at[o], across)
        started += x_across[o] + [x_twin[o], x_far[o], p_twin[o], p_across[o]]

    def line_out(o):
        line_sems[o] = sems(LINE - 1)
        for m in range(1, LINE):
            index = line_sems[o] + m - 1
            block = xin.at[0, held(o, i)]
            out = copy(block, block, index, index, peers[m - 1])
            out.start()
            started.append(out)
        x_across[o][0].start()

    def line_in(o):
        for m in range(1, LINE):
            arrived(xin.at[0, held(o, (i + LINE - m) % LINE)], line_sems[o] + m - 1)
            x_across[o][m].start()
        x_twin[o].start()

    def pass_on(o):
        for part in x_across[o]:
            part.wait_recv()
        x_far[o].start()

    def experts(o):
        x_twin[o].wait_recv()
        x_far[o].wait_recv()
        rows = xin[:, o * LINE : (o + 1) * LINE].reshape(256, q)
        sorted_rows = jnp.dot(gather[...], rows, preferred_element_type=F32).astype(BF16)
        projected = jnp.zeros((64, wgu.shape[1]), F32)
        for n in range(QUARTERS):
            projected += jnp.dot(
                sorted_rows[n * 64 : (n + 1) * 64],
                wgu[n * q : (n + 1) * q],
                preferred_element_type=F32,
            )
        gate, upper = projected[:, :128], projected[:, 128:]
        hidden = (gate * jax.nn.sigmoid(gate) * upper).astype(BF16)
        part = jnp.dot(hidden, wd[...], preferred_element_type=F32)
        p_send[o, 0] = part[16:32].astype(BF16)
        p_send[o, 1] = part[48:64].astype(BF16)
        p_twin[o].start()
        p_own[o, 0] = part[0:16]
        p_own[o, 1] = part[32:48]

    def sum_twins(o):
        p_twin[o].wait_recv()
        y_send[o] = (p_own[o, 1] + p_recv[o, 1].astype(F32)).astype(BF16)
        p_across[o].start()
        p_own[o, 0] = p_own[o, 0] + p_recv[o, 0].astype(F32)

    def to_blocks(o):
        p_across[o].wait_recv()
        total = (p_own[o, 0] + y_recv[o].astype(F32)).astype(BF16)
        stacked = jnp.concatenate([total[:, n * q : (n + 1) * q] for n in range(QUARTERS)], axis=0)
        blocks = jnp.dot(scatter[...], stacked, preferred_element_type=F32).astype(BF16)
        line_send[o] = blocks.reshape(LINE, 16, q)

    back_sems = {}

    def line_back(o):
        back_sems[o] = sems(LINE - 1)
        for m in range(1, LINE):
            index = back_sems[o] + m - 1
            block = held(o, (i + m) % LINE) - o * LINE
            out = copy(line_send.at[o, block], line_recv.at[o, m - 1], index, index, peers[m - 1])
            out.start()
            started.append(out)

    def line_sum(o):
        total = line_send[o, held(o, i) - o * LINE].astype(F32)
        for m in range(1, LINE):
            arrived(line_recv.at[o, m - 1], back_sems[o] + m - 1)
            total = total + line_recv[o, m - 1].astype(F32)
        return total.astype(BF16)

    line_out(0)

    @pl.when(core == 1)
    def _():
        pl.semaphore_wait(barrier, far)
        signal(met, twin)

    @pl.when(core == 0)
    def _():
        pl.semaphore_wait(met, 1)

    far_opp.start()
    far_plus.start()
    far_minus.start()
    line_in(0)
    far_minus.wait_recv()
    line_out(1)
    far_plus.wait_recv()
    line_out(3)
    far_opp.wait_recv()
    line_out(2)
    pass_on(0)
    experts(0)
    line_in(1)
    line_in(3)
    line_in(2)
    sum_twins(0)
    pass_on(1)
    experts(1)
    pass_on(3)
    experts(3)
    to_blocks(0)
    line_back(0)
    sum_twins(1)
    sum_twins(3)
    pass_on(2)
    experts(2)
    sum_twins(2)
    to_blocks(1)
    line_back(1)
    to_blocks(3)
    line_back(3)
    to_blocks(2)
    line_back(2)

    returns = []
    for o, slot, device in ((1, 2, plus4), (3, 0, minus4), (2, 1, opposite)):
        far_send[o - 1] = line_sum(o)
        returns.append(plain(far_send.at[o - 1], far_recv.at[slot], device))
        returns[-1].start()
    started += returns

    own_sum[...] = line_sum(0)

    pl.when(not_last)(relay_up.wait_send)
    pl.when(not_first)(relay_down.wait_send)
    for out in started:
        out.wait_send()

    for out in returns:
        out.wait_recv()
    parts = jnp.concatenate([own_sum[...]] + [far_recv[n] for n in range(3)], axis=0)
    added = jnp.dot(mixing, jnp.concatenate([parts, parts], axis=0), preferred_element_type=F32)
    mixed = current[...].reshape(32, q).astype(F32) + added
    for s in range(2):
        for n in range(QUARTERS):
            first = s * 16 + n * TOK
            result[s, :, n * q : (n + 1) * q] = mixed[first : first + TOK].astype(BF16)


def shards(ns, *args):
    tokens_a = args[0]
    d = tokens_a.shape[1]
    q = d // QUARTERS
    width = args[7].shape[1]
    vmem = pl.BlockSpec(memory_space=pltpu.VMEM)
    smem = pl.BlockSpec(memory_space=pltpu.SMEM)
    hbm = pl.BlockSpec(memory_space=pl.ANY)
    small = [array.T for array in args[2:6]]
    mixed = pl.pallas_call(
        functools.partial(kernel, ns, d),
        out_shape=jax.ShapeDtypeStruct((2,) + tokens_a.shape, BF16),
        in_specs=[vmem] * 2 + [smem] * 4 + [hbm] * 2,
        out_specs=vmem,
        scratch_shapes=[
            pltpu.VMEM((2, 16, q), BF16),
            pltpu.VMEM((2, 16, q), BF16),
            pltpu.VMEM((3, 16, q), BF16),
            pltpu.VMEM((4, NZ, 16, q), BF16),
            pltpu.VMEM((d, 2, width), BF16),
            pltpu.VMEM((d, 2 * width), BF16),
            pltpu.VMEM((width, d), BF16),
            pltpu.VMEM((256, 256), BF16),
            pltpu.VMEM((64, 64), BF16),
            pltpu.VMEM((EXPERTS, 2, 16, d), F32),
            pltpu.VMEM((EXPERTS, 2, 16, d), BF16),
            pltpu.VMEM((EXPERTS, 2, 16, d), BF16),
            pltpu.VMEM((EXPERTS, 16, d), BF16),
            pltpu.VMEM((EXPERTS, 16, d), BF16),
            pltpu.VMEM((EXPERTS, LINE, 16, q), BF16),
            pltpu.VMEM((EXPERTS, LINE - 1, 16, q), BF16),
            pltpu.VMEM((3, 16, q), BF16),
            pltpu.VMEM((3, 16, q), BF16),
            pltpu.VMEM((16, q), BF16),
            pltpu.SemaphoreType.DMA((N_SEMS,)),
            pltpu.SemaphoreType.DMA((N_SEMS,)),
            pltpu.SemaphoreType.DMA((2,)),
            pltpu.SemaphoreType.REGULAR,
        ],
        compiler_params=pltpu.CompilerParams(
            collective_id=0, has_side_effects=True, vmem_limit_bytes=60 * 1024 * 1024
        ),
    )(*args[:2], *small, *args[6:])
    return mixed[0], mixed[1]


def solution(mesh):
    ns = mesh.shape["section"]
    rows = P(("section", "ep"), None)
    in_specs = (rows,) * 6 + (P("section", None, None, "ep"), P("section", "ep", None))
    return jax.shard_map(
        functools.partial(shards, ns),
        mesh=mesh,
        in_specs=in_specs,
        out_specs=(rows, rows),
        check_vma=False,
    )
```

```python
import functools

import jax
import jax.numpy as jnp
from jax import lax
from jax.experimental import pallas as pl
from jax.experimental.pallas import tpu as pltpu
from jax.sharding import PartitionSpec as P

EXPERTS = 4
TOP = 2
TOK = 4
CAP = 2
QUARTERS = 4
LINE = 4
NZ = EXPERTS * LINE
BF16 = jnp.bfloat16
F32 = jnp.float32
MESH = pl.DeviceIdType.MESH
N_SEMS = 80


def iota(shape, dim):
    return lax.broadcasted_iota(jnp.int32, shape, dim)


def find_tokens(routes, gains, stream, expert, slot):
    count = jnp.zeros(stream.shape, jnp.int32)
    token = jnp.zeros(stream.shape, jnp.int32)
    gain = jnp.zeros(stream.shape, F32)
    for t in range(TOK):
        for k in range(TOP):
            route = jnp.where(stream == 0, routes[0][k, t], routes[1][k, t])
            named = route == expert
            here = named & (count == slot)
            token = jnp.where(here, t, token)
            if gains is not None:
                value = jnp.where(stream == 0, gains[0][k, t], gains[1][k, t])
                gain = jnp.where(here, value, gain)
            count = count + named.astype(jnp.int32)
    return token, gain


def kernel(
    ns,
    d,
    tok_a,
    tok_b,
    routes_a,
    routes_b,
    gains_a,
    gains_b,
    wgu_hbm,
    wd_hbm,
    result,
    outgoing,
    current,
    packed,
    xin,
    wgu_raw,
    wgu,
    wd,
    gather,
    scatter,
    p_own,
    p_send,
    p_recv,
    y_send,
    y_recv,
    line_send,
    line_recv,
    far_send,
    far_recv,
    own_sum,
    send_sems,
    recv_sems,
    local_sems,
    met,
):
    q = d // QUARTERS
    section = lax.axis_index("section")
    ep = lax.axis_index("ep")
    z, low = ep // 4, ep % 4
    y, core = low // 2, low % 2
    g, i = z // LINE, z % LINE

    def at(to_z):
        return (section, to_z * 4 + low)

    plus4, minus4 = at((z + LINE) % NZ), at((z + NZ - LINE) % NZ)
    opposite_z = LINE * ((g + 2) % EXPERTS) + LINE - 1 - i
    opposite = at(opposite_z)
    peers = [at(g * LINE + (i + m) % LINE) for m in range(1, LINE)]
    across = (section, ep + 2 - 4 * y)
    twin = (section, ep + 1 - 2 * core)
    up, down = (section + 1, ep), (section - 1, ep)
    not_last, not_first = section < ns - 1, section > 0

    load_gu = pltpu.make_async_copy(wgu_hbm.at[0], wgu_raw, local_sems.at[0])
    load_d = pltpu.make_async_copy(wd_hbm.at[0], wd, local_sems.at[1])

    barrier = pltpu.get_barrier_semaphore()

    def signal(semaphore, device):
        pl.semaphore_signal(semaphore, inc=1, device_id=device, device_id_type=MESH)

    def greet(to_section, to_z, to_y, to_core):
        signal(barrier, (to_section, to_z * 4 + to_y * 2 + to_core))

    greet(section, opposite_z, y, 1)
    greet(section, (z + LINE) % NZ, y, 1)
    greet(section, (z + NZ - LINE) % NZ, y, 1)
    pl.when(not_last)(lambda: greet(section + 1, z, y, 0))
    pl.when(not_first)(lambda: greet(section - 1, z, y, 0))
    for m in range(1, LINE):
        greet(section, g * LINE + (i + m) % LINE, y, 0)
    greet(section, z, 1 - y, 0)
    signal(barrier, twin)
    load_gu.start()
    load_d.start()

    used = [0]

    def sems(n=1):
        used[0] += n
        return used[0] - n

    def copy(src, dst, send_index, recv_index, device):
        return pltpu.make_async_remote_copy(
            src_ref=src,
            dst_ref=dst,
            send_sem=send_sems.at[send_index],
            recv_sem=recv_sems.at[recv_index],
            device_id=device,
            device_id_type=MESH,
        )

    def plain(src, dst, device):
        index = sems()
        return copy(src, dst, index, index, device)

    def arrived(dst, recv_index):
        copy(dst, dst, 0, recv_index, twin).wait_recv()

    for stream, tok in enumerate((tok_a, tok_b)):
        rows = tok[...].astype(F32)
        outgoing[stream] = jnp.concatenate(
            [rows[:, n * q : (n + 1) * q] for n in range(QUARTERS)], axis=0
        ).astype(BF16)

    relay_up = plain(outgoing.at[0], current.at[0], up)
    relay_down = plain(outgoing.at[1], current.at[1], down)

    near = 2 * (LINE + not_last.astype(jnp.int32) + not_first.astype(jnp.int32)) + 1
    far = 2 * 3 + 1

    @pl.when(core == 0)
    def _():
        pl.semaphore_wait(barrier, near)
        signal(met, twin)

    @pl.when(core == 1)
    def _():
        pl.semaphore_wait(met, 1)

    pl.when(not_last)(relay_up.start)
    pl.when(not_first)(relay_down.start)

    @pl.when(section == 0)
    def _():
        current[0] = outgoing[0]

    @pl.when(section == ns - 1)
    def _():
        current[1] = outgoing[1]

    row, col = iota((64, 32), 0), iota((64, 32), 1)
    token, _ = find_tokens(
        (routes_a, routes_b), None, (row // 2) % 2, (g + row // 16) % EXPERTS, row % CAP
    )
    place = ((row // 2) % 2) * 16 + ((row // 4) % 4) * 4 + token
    picker = jnp.where(col == place, 1.0, 0.0).astype(BF16)

    lane = iota((1, 128), 1)
    token, gain = find_tokens(
        (routes_a, routes_b),
        (gains_a, gains_b),
        (lane // 2) % 2,
        (g + (lane // 16) % 4) % EXPERTS,
        lane % CAP,
    )
    high = gain.astype(BF16).astype(F32)
    weight = jnp.where(lane < 64, high, gain - high)
    row = iota((32, 128), 0)
    mine = (row % 4 == token) & ((row // 4) % 4 == (lane // 4) % 4) & (row // 16 == (lane // 2) % 2)
    mixing = jnp.where(mine, weight, 0.0).astype(BF16)

    row, col = iota((256, 256), 0), iota((256, 256), 1)
    place = ((row // 16) % 4) * 64 + ((row // 4) % 4) * 16 + (row // 64) * 4 + row % 4
    gather[...] = jnp.where(col == place, 1.0, 0.0).astype(BF16)
    row, col = iota((64, 64), 0), iota((64, 64), 1)
    place = ((row // 4) % 4) * 16 + (row // 16) * 4 + row % 4
    scatter[...] = jnp.where(col == place, 1.0, 0.0).astype(BF16)

    load_gu.wait()

    def unpack_weights(n, carry):
        rows = pl.ds(pl.multiple_of(n * 256, 256), 256)
        wgu[rows, :] = wgu_raw[rows].reshape(256, wgu.shape[1])
        return carry

    lax.fori_loop(0, d // 256, unpack_weights, 0)
    load_d.wait()

    pl.when(not_first)(relay_up.wait_recv)
    pl.when(not_last)(relay_down.wait_recv)

    picked = jnp.dot(picker, current[...].reshape(32, q), preferred_element_type=F32).astype(BF16)
    xin[0, i] = picked[0:16]
    packed[0] = picked[32:48]
    packed[1] = picked[16:32]
    packed[2] = picked[48:64]
    far_opp = plain(packed.at[0], xin.at[0, 2 * LINE + i], opposite)
    far_plus = plain(packed.at[1], xin.at[0, 3 * LINE + i], plus4)
    far_minus = plain(packed.at[2], xin.at[0, LINE + i], minus4)
    started = [far_opp, far_plus, far_minus]

    def held(o, j):
        return 2 * LINE + LINE - 1 - j if o == 2 else o * LINE + j

    x_across, x_twin, x_far, p_twin, p_across, line_sems = {}, {}, {}, {}, {}, {}
    for o in range(EXPERTS):
        block = pl.ds(o * LINE, LINE)
        x_across[o] = []
        for m in range(LINE):
            place = held(o, (i + LINE - m) % LINE)
            x_across[o].append(plain(xin.at[0, place], xin.at[2, place], across))
        x_twin[o] = plain(xin.at[0, block], xin.at[1, block], twin)
        x_far[o] = plain(xin.at[2, block], xin.at[3, block], twin)
        p_twin[o] = plain(p_send.at[o], p_recv.at[o], twin)
        p_across[o] = plain(y_send.at[o], y_recv.at[o], across)
        started += x_across[o] + [x_twin[o], x_far[o], p_twin[o], p_across[o]]

    def line_out(o):
        line_sems[o] = sems(LINE - 1)
        for m in range(1, LINE):
            index = line_sems[o] + m - 1
            block = xin.at[0, held(o, i)]
            out = copy(block, block, index, index, peers[m - 1])
            out.start()
            started.append(out)
        x_across[o][0].start()

    def line_in(o):
        for m in range(1, LINE):
            arrived(xin.at[0, held(o, (i + LINE - m) % LINE)], line_sems[o] + m - 1)
            x_across[o][m].start()
        x_twin[o].start()

    def pass_on(o):
        for part in x_across[o]:
            part.wait_recv()
        x_far[o].start()

    def experts(o):
        x_twin[o].wait_recv()
        x_far[o].wait_recv()
        rows = xin[:, o * LINE : (o + 1) * LINE].reshape(256, q)
        sorted_rows = jnp.dot(gather[...], rows, preferred_element_type=F32).astype(BF16)
        projected = jnp.zeros((64, wgu.shape[1]), F32)
        for n in range(QUARTERS):
            projected += jnp.dot(
                sorted_rows[n * 64 : (n + 1) * 64],
                wgu[n * q : (n + 1) * q],
                preferred_element_type=F32,
            )
        gate, upper = projected[:, :128], projected[:, 128:]
        hidden = (gate * jax.nn.sigmoid(gate) * upper).astype(BF16)
        part = jnp.dot(hidden, wd[...], preferred_element_type=F32)
        p_send[o, 0] = part[16:32].astype(BF16)
        p_send[o, 1] = part[48:64].astype(BF16)
        p_twin[o].start()
        p_own[o, 0] = part[0:16]
        p_own[o, 1] = part[32:48]

    def sum_twins(o):
        p_twin[o].wait_recv()
        y_send[o] = (p_own[o, 1] + p_recv[o, 1].astype(F32)).astype(BF16)
        p_across[o].start()
        p_own[o, 0] = p_own[o, 0] + p_recv[o, 0].astype(F32)

    def to_blocks(o):
        p_across[o].wait_recv()
        total = (p_own[o, 0] + y_recv[o].astype(F32)).astype(BF16)
        stacked = jnp.concatenate([total[:, n * q : (n + 1) * q] for n in range(QUARTERS)], axis=0)
        blocks = jnp.dot(scatter[...], stacked, preferred_element_type=F32).astype(BF16)
        line_send[o] = blocks.reshape(LINE, 16, q)

    back_sems = {}

    def line_back(o):
        back_sems[o] = sems(LINE - 1)
        for m in range(1, LINE):
            index = back_sems[o] + m - 1
            block = held(o, (i + m) % LINE) - o * LINE
            out = copy(line_send.at[o, block], line_recv.at[o, m - 1], index, index, peers[m - 1])
            out.start()
            started.append(out)

    def line_sum(o):
        total = line_send[o, held(o, i) - o * LINE].astype(F32)
        for m in range(1, LINE):
            arrived(line_recv.at[o, m - 1], back_sems[o] + m - 1)
            total = total + line_recv[o, m - 1].astype(F32)
        return total.astype(BF16)

    line_out(0)

    @pl.when(core == 1)
    def _():
        pl.semaphore_wait(barrier, far)
        signal(met, twin)

    @pl.when(core == 0)
    def _():
        pl.semaphore_wait(met, 1)

    far_opp.start()
    far_plus.start()
    far_minus.start()
    line_in(0)
    far_minus.wait_recv()
    line_out(1)
    far_plus.wait_recv()
    line_out(3)
    far_opp.wait_recv()
    line_out(2)
    pass_on(0)
    experts(0)
    line_in(1)
    line_in(3)
    line_in(2)
    sum_twins(0)
    pass_on(1)
    experts(1)
    pass_on(3)
    experts(3)
    to_blocks(0)
    line_back(0)
    sum_twins(1)
    sum_twins(3)
    pass_on(2)
    experts(2)
    sum_twins(2)
    to_blocks(1)
    line_back(1)
    to_blocks(3)
    line_back(3)
    to_blocks(2)
    line_back(2)

    returns = []
    for o, slot, device in ((1, 2, plus4), (3, 0, minus4), (2, 1, opposite)):
        far_send[o - 1] = line_sum(o)
        returns.append(plain(far_send.at[o - 1], far_recv.at[slot], device))
        returns[-1].start()
    started += returns

    own_sum[...] = line_sum(0)

    pl.when(not_last)(relay_up.wait_send)
    pl.when(not_first)(relay_down.wait_send)
    for out in started:
        out.wait_send()

    def mix(weights, part):
        twice = jnp.concatenate([part, part], axis=0)
        return jnp.dot(weights, twice, preferred_element_type=F32)

    def weights_of(first, last):
        return jnp.concatenate([mixing[:, first:last], mixing[:, 64 + first : 64 + last]], axis=1)

    late = weights_of(32, 48)
    returns[0].wait_recv()
    returns[1].wait_recv()
    parts = jnp.concatenate([own_sum[...], far_recv[0], far_recv[2]], axis=0)
    early = jnp.concatenate([weights_of(0, 32), weights_of(48, 64)], axis=1)
    parts = jnp.concatenate([parts[0:32], parts[0:32], parts[32:48], parts[32:48]], axis=0)
    mixed = current[...].reshape(32, q).astype(F32)
    mixed = mixed + jnp.dot(early, parts, preferred_element_type=F32)
    returns[2].wait_recv()
    mixed = mixed + mix(late, far_recv[1])
    for s in range(2):
        for n in range(QUARTERS):
            first = s * 16 + n * TOK
            result[s, :, n * q : (n + 1) * q] = mixed[first : first + TOK].astype(BF16)


def shards(ns, *args):
    tokens_a = args[0]
    d = tokens_a.shape[1]
    q = d // QUARTERS
    width = args[7].shape[1]
    vmem = pl.BlockSpec(memory_space=pltpu.VMEM)
    smem = pl.BlockSpec(memory_space=pltpu.SMEM)
    hbm = pl.BlockSpec(memory_space=pl.ANY)
    small = [array.T for array in args[2:6]]
    mixed = pl.pallas_call(
        functools.partial(kernel, ns, d),
        out_shape=jax.ShapeDtypeStruct((2,) + tokens_a.shape, BF16),
        in_specs=[vmem] * 2 + [smem] * 4 + [hbm] * 2,
        out_specs=vmem,
        scratch_shapes=[
            pltpu.VMEM((2, 16, q), BF16),
            pltpu.VMEM((2, 16, q), BF16),
            pltpu.VMEM((3, 16, q), BF16),
            pltpu.VMEM((4, NZ, 16, q), BF16),
            pltpu.VMEM((d, 2, width), BF16),
            pltpu.VMEM((d, 2 * width), BF16),
            pltpu.VMEM((width, d), BF16),
            pltpu.VMEM((256, 256), BF16),
            pltpu.VMEM((64, 64), BF16),
            pltpu.VMEM((EXPERTS, 2, 16, d), F32),
            pltpu.VMEM((EXPERTS, 2, 16, d), BF16),
            pltpu.VMEM((EXPERTS, 2, 16, d), BF16),
            pltpu.VMEM((EXPERTS, 16, d), BF16),
            pltpu.VMEM((EXPERTS, 16, d), BF16),
            pltpu.VMEM((EXPERTS, LINE, 16, q), BF16),
            pltpu.VMEM((EXPERTS, LINE - 1, 16, q), BF16),
            pltpu.VMEM((3, 16, q), BF16),
            pltpu.VMEM((3, 16, q), BF16),
            pltpu.VMEM((16, q), BF16),
            pltpu.SemaphoreType.DMA((N_SEMS,)),
            pltpu.SemaphoreType.DMA((N_SEMS,)),
            pltpu.SemaphoreType.DMA((2,)),
            pltpu.SemaphoreType.REGULAR,
        ],
        compiler_params=pltpu.CompilerParams(
            collective_id=0, has_side_effects=True, vmem_limit_bytes=60 * 1024 * 1024
        ),
    )(*args[:2], *small, *args[6:])
    return mixed[0], mixed[1]


def solution(mesh):
    ns = mesh.shape["section"]
    rows = P(("section", "ep"), None)
    in_specs = (rows,) * 6 + (P("section", None, None, "ep"), P("section", "ep", None))
    return jax.shard_map(
        functools.partial(shards, ns),
        mesh=mesh,
        in_specs=in_specs,
        out_specs=(rows, rows),
        check_vma=False,
    )
```
